32 devices in a mesh: dom: 2 (over x), fsdp: 8 (over z, y), dp: 2 (over core).
Axes of the slice: x: 2, y: 2, z: 4, core: 2. Of those that a mesh axis runs over, the one named last changes fastest.
Arguments:
- activations: bfloat16 [4096, 8192], P(('dom', 'fsdp', 'dp')), parts along dimension 0, may hold values from -6 to 6
- cotangents: bfloat16 [4096, 8192], P(('dom', 'fsdp', 'dp')), parts along dimension 0, may hold values from -6 to 6
- in_factor: bfloat16 [8192, 64], replicated, may hold values from -0.0625 to 0.0625
- out_factor: bfloat16 [8192, 128], replicated, may hold values from -0.0625 to 0.0625
- earlier: bfloat16 [1024, 8192], P(('dom', 'fsdp', 'dp')), parts along dimension 0, may hold values from -6 to 6
Outputs:
- features: bfloat16 [32, 8192], P(('dom', 'fsdp', 'dp')), parts along dimension 0
- gram: float32 [16384, 8192], P(('dom', 'fsdp', 'dp')), parts along dimension 0
The draws below stay inside these ranges and needn't reach their ends.
There are 2 independent parts, one for each index of `dom`. The reference program is written for one: setup_inputs(seed, part) draws one part's arguments, and reference() takes and returns one part's arrays. A program takes and returns all parts, laid end to end along the dimension named above; an argument that names none is the same for every part. Nothing has to cross between parts.
All inputs are finite; a program needn't handle non-finite values.
Results may differ from the reference program's by a relative error of at most 0.0058.
Values may be sent and summed in bfloat16 or wider, within the bound.
A program may use at most 192 MiB of HBM per device.

```python
import jax
import jax.numpy as jnp

D = 8192
KIN = 64
KOUT = 128
LEN = 128
FEAT = 8192
SEQS = 16
TOKENS = 2048
PREV_TOTAL = 512


def levels(own_key, shape, split, low, high):
    factor_of, own = 1.0, jax.random.fold_in(own_key, 6)
    for dim, shards_of in split:
        heights = jnp.exp(jax.random.uniform(jax.random.fold_in(own, dim), (shards_of,), jnp.float32, low / len(split), high / len(split)))
        factor_of = factor_of * jnp.repeat(heights, shape[dim] // shards_of).reshape([-1 if axis == dim else 1 for axis in range(len(shape))])
    return factor_of


def bell_draw(own_key, extent, width, reach, cuts=(), held_as=jnp.bfloat16):
    entries = width * jax.random.normal(own_key, extent, jnp.float32)
    if cuts:
        entries = entries * levels(own_key, extent, cuts, -0.22, 0.18)
    return jnp.clip(entries, -reach, reach).astype(held_as)


def setup_inputs(seed: int = 0, part: int = 0) -> dict:
    streams_of = jax.random.split(jax.random.key(seed), 6)
    own_keys = jax.random.split(jax.random.fold_in(streams_of[5], part), 6)
    activations = bell_draw(own_keys[0], (TOKENS, D), 1.0, 6.0, ((0, 16),))
    cotangents = bell_draw(own_keys[1], (TOKENS, D), 1.0, 6.0, ((0, 16),))
    in_factor = bell_draw(streams_of[2], (D, KIN), D ** -0.5, 0.0625)
    out_factor = bell_draw(streams_of[3], (D, KOUT), D ** -0.5, 0.0625)
    earlier = bell_draw(own_keys[4], (PREV_TOTAL, FEAT), 1.0, 6.0, ((0, 16),))
    return dict(activations=activations, cotangents=cotangents, in_factor=in_factor, out_factor=out_factor, earlier=earlier)


def reference(activations, cotangents, in_factor, out_factor, earlier):
    inner = jnp.dot(activations, in_factor, preferred_element_type=jnp.float32).astype(jnp.bfloat16)
    outer = jnp.dot(cotangents, out_factor, preferred_element_type=jnp.float32).astype(jnp.bfloat16)
    outer3 = outer.reshape(SEQS, LEN, KOUT).astype(jnp.float32)
    inner3 = inner.reshape(SEQS, LEN, KIN).astype(jnp.float32)
    blocks = jnp.einsum("sta,stb->sab", outer3, inner3)
    features = (blocks.reshape(SEQS, KOUT * KIN) * (LEN ** -0.5)).astype(jnp.bfloat16)
    summed = jnp.dot(earlier.T, earlier, preferred_element_type=jnp.float32)
    gram = summed / PREV_TOTAL
    return features, gram
```

```python
import functools

import jax
import jax.numpy as jnp
from jax import lax
from jax.experimental import pallas as pl
from jax.experimental.pallas import tpu as pltpu
from jax.sharding import PartitionSpec as P

LEN = 128
AXES = ("fsdp", "dp")
MIB = 1 << 20
CHUNKS = 4
DEPTH = 4
SIDES = 2


def gather_kernel(act_ref, cot_ref, inf_ref, outf_ref, own_ref, all_ref, feat_ref,
                  act, cot, inf, outf, flat, blk, up_sem, down_sem, side_sem, core_sem,
                  ici_sem, pair_sem, own_sem, load_sem):
    dom, f, c = lax.axis_index("dom"), lax.axis_index("fsdp"), lax.axis_index("dp")
    z, y = f // SIDES, f % SIDES
    rows, width = own_ref.shape
    step = width // CHUNKS
    last = DEPTH - 1
    far = range(CHUNKS // 2)
    near = range(CHUNKS // 2, CHUNKS)

    def device(zz, yy, cc):
        return (dom, zz * SIDES + yy, cc)

    up, down = device(jnp.minimum(z + 1, last), y, c), device(jnp.maximum(z - 1, 0), y, c)
    side, pair = device(z, 1 - y, c), device(z, y, 1 - c)
    has_up, has_down = z < last, z > 0

    loads = [pltpu.make_async_copy(s, d, load_sem.at[i])
             for i, (s, d) in enumerate(((act_ref, act), (cot_ref, cot), (inf_ref, inf), (outf_ref, outf)))]
    for copy in loads:
        copy.start()

    barrier = pltpu.get_barrier_semaphore()

    def greet(to):
        pl.semaphore_signal(barrier, inc=1, device_id=to, device_id_type=pl.DeviceIdType.MESH)

    pl.when(has_up)(lambda: greet(up))
    pl.when(has_down)(lambda: greet(down))
    greet(side)
    greet(pair)
    pl.semaphore_wait(barrier, 2 + has_up.astype(jnp.int32) + has_down.astype(jnp.int32))

    def place(ff, cc, k):
        start = pl.multiple_of((ff * 2 + cc) * rows, rows)
        return all_ref.at[pl.ds(start, rows), pl.ds(k * step, step)]

    def send(sems, ff, k, to, own=False):
        src = own_ref.at[:, pl.ds(k * step, step)] if own else place(ff, c, k)
        recv = pair_sem if sems is core_sem else ici_sem
        return pltpu.make_async_remote_copy(
            src_ref=src, dst_ref=place(ff, c, k), send_sem=sems.at[ff, k], recv_sem=recv.at[ff, k],
            device_id=to, device_id_type=pl.DeviceIdType.MESH)

    sent = []

    def go(sems, ff, k, to, cond=None, own=False):
        copy = send(sems, ff, k, to, own)
        if cond is None:
            copy.start()
        else:
            pl.when(cond)(lambda: copy.start())
        sent.append((cond, copy))

    def arrive(ff, k, cond):
        pl.when(cond)(lambda: send(side_sem, ff, k, side).wait_recv())

    keep = pltpu.make_async_copy(own_ref, all_ref.at[pl.ds(pl.multiple_of((f * 2 + c) * rows, rows), rows)], own_sem)
    for k in range(CHUNKS):
        go(up_sem, f, k, up, has_up, True)
        go(down_sem, f, k, down, has_down, True)
        go(side_sem, f, k, side, None, True)
    for k in range(CHUNKS):
        go(core_sem, f, k, pair, None, True)
    keep.start()

    for copy in loads:
        copy.wait()
    kin, kout = inf.shape[1], outf.shape[1]
    part = width // 8

    def project(i, totals):
        at = pl.ds(pl.multiple_of(i * part, part), part)
        return (totals[0] + jnp.dot(act[:, at], inf[at, :], preferred_element_type=jnp.float32),
                totals[1] + jnp.dot(cot[:, at], outf[at, :], preferred_element_type=jnp.float32))

    inner, outer = lax.fori_loop(0, 8, project, (jnp.zeros((LEN, kin), jnp.float32), jnp.zeros((LEN, kout), jnp.float32)))
    inner, outer = inner.astype(jnp.bfloat16), outer.astype(jnp.bfloat16)
    blk[...] = lax.dot_general(outer, inner, (((0,), (0,)), ((), ())), preferred_element_type=jnp.float32) * LEN ** (-0.5)
    wide = jnp.concatenate([blk[pl.ds(0, kout // 2, 2), :], blk[pl.ds(1, kout // 2, 2), :]], axis=1)
    for a in range(kout // 2):
        flat[0:1, 2 * kin * a:2 * kin * (a + 1)] = wide[a:a + 1, :]
    feat_ref[...] = flat[...].astype(feat_ref.dtype)

    def beside(ff):
        return ff + 1 - 2 * y

    for s in range(1, DEPTH + 1):
        below, above = z - s, z + s
        f_below, f_above = jnp.maximum(below, 0) * SIDES + y, jnp.minimum(above, last) * SIDES + y
        if s <= last:
            has_b, has_a = below >= 0, above <= last
            for k in range(CHUNKS):
                arrive(f_below, k, has_b)
                go(up_sem, f_below, k, up, has_b & has_up)
                across = has_b & (below != 0) if k in far else has_b
                go(side_sem, f_below, k, side, across)
                go(core_sem, f_below, k, pair, has_b)
                arrive(f_above, k, has_a)
                go(down_sem, f_above, k, down, has_a & has_down)
                across = has_a & (above != last) if k in far else has_a
                go(side_sem, f_above, k, side, across)
                go(core_sem, f_above, k, pair, has_a)
        for ff, here, to, on, sems in ((0 * SIDES + 1 - y, z == s - 1, up, has_up, up_sem),
                                       (last * SIDES + 1 - y, z == last - (s - 1), down, has_down, down_sem)):
            for k in far:
                arrive(ff, k, here)
                go(sems, ff, k, to, here & on)
                go(core_sem, ff, k, pair, here)
        d = s - 1
        for k in (*near, *far):
            for zz in ((z,) if d == 0 else (z - d, z + d)):
                ok = (zz >= 0) & (zz <= last)
                if k in far:
                    ok = ok & (zz != 0) & (zz != last)
                ff = jnp.clip(zz, 0, last) * SIDES + 1 - y
                arrive(ff, k, ok)
                go(core_sem, ff, k, pair, ok)

    for cond, copy in sent:
        if cond is None:
            copy.wait_send()
        else:
            pl.when(cond)(lambda copy=copy: copy.wait_send())
    keep.wait()
    for ff in range(DEPTH * SIDES):
        for k in range(CHUNKS):
            pltpu.make_async_remote_copy(
                src_ref=place(ff, 1 - c, k), dst_ref=place(ff, 1 - c, k), send_sem=core_sem.at[ff, k],
                recv_sem=pair_sem.at[ff, k], device_id=pair, device_id_type=pl.DeviceIdType.MESH).wait_recv()


def gather(activations, cotangents, in_factor, out_factor, earlier):
    rows, width = earlier.shape
    devices = DEPTH * SIDES * 2
    kin, kout = in_factor.shape[1], out_factor.shape[1]
    hbm = pl.BlockSpec(memory_space=pl.ANY)
    dma = pltpu.SemaphoreType.DMA
    chips = DEPTH * SIDES
    return pl.pallas_call(
        gather_kernel,
        name="gather_and_features",
        out_shape=(jax.ShapeDtypeStruct((rows * devices, width), earlier.dtype),
                   jax.ShapeDtypeStruct((1, kin * kout), jnp.bfloat16)),
        in_specs=[hbm] * 5,
        out_specs=(hbm, pl.BlockSpec(memory_space=pltpu.VMEM)),
        scratch_shapes=[
            pltpu.VMEM(activations.shape, activations.dtype),
            pltpu.VMEM(cotangents.shape, cotangents.dtype),
            pltpu.VMEM(in_factor.shape, in_factor.dtype),
            pltpu.VMEM(out_factor.shape, out_factor.dtype),
            pltpu.VMEM((1, kin * kout), jnp.float32),
            pltpu.VMEM((kout, kin), jnp.float32),
            *[dma((chips, CHUNKS))] * 6,
            dma(()),
            dma((4,)),
        ],
        compiler_params=pltpu.CompilerParams(collective_id=1, has_side_effects=True, vmem_limit_bytes=24 * MIB),
    )(activations, cotangents, in_factor, out_factor, earlier)


def gram_kernel(scale, cols_ref, tile_ref, feat_ref, gram_ref, out_feat_ref, turned):
    @pl.when(pl.program_id(0) == 0)
    def _():
        turned[...] = cols_ref[...].T
        out_feat_ref[...] = feat_ref[...]

    gram_ref[...] = jnp.dot(turned[...], tile_ref[...], preferred_element_type=jnp.float32) * scale


def gram_of(everything, features):
    total, width = everything.shape
    assert total & (total - 1) == 0
    owned = width // (lax.axis_size("fsdp") * lax.axis_size("dp"))
    tile = 1024
    whole = pl.BlockSpec(features.shape, lambda j: (0, 0))
    return pl.pallas_call(
        functools.partial(gram_kernel, 1.0 / total),
        name="gram",
        grid=(width // tile,),
        out_shape=(jax.ShapeDtypeStruct((owned, width), jnp.float32),
                   jax.ShapeDtypeStruct(features.shape, features.dtype)),
        in_specs=[pl.BlockSpec((total, owned), lambda j: (0, lax.axis_index("fsdp") * 2 + lax.axis_index("dp"))),
                  pl.BlockSpec((total, tile), lambda j: (0, j)), whole],
        out_specs=(pl.BlockSpec((owned, tile), lambda j: (0, j)), whole),
        scratch_shapes=[pltpu.VMEM((owned, total), everything.dtype)],
        compiler_params=pltpu.CompilerParams(vmem_limit_bytes=24 * MIB),
    )(everything, everything, features)


def plain_features(activations, cotangents, in_factor, out_factor):
    inner = jnp.dot(activations, in_factor, preferred_element_type=jnp.float32).astype(jnp.bfloat16)
    outer = jnp.dot(cotangents, out_factor, preferred_element_type=jnp.float32).astype(jnp.bfloat16)
    kin, kout = inner.shape[1], outer.shape[1]
    blocks = jnp.einsum("sta,stb->sab", outer.reshape(-1, LEN, kout), inner.reshape(-1, LEN, kin),
                        preferred_element_type=jnp.float32)
    return (blocks.reshape(-1, kout * kin) * LEN ** (-0.5)).astype(jnp.bfloat16)


def on_device(activations, cotangents, in_factor, out_factor, earlier):
    if lax.axis_size("fsdp") == DEPTH * SIDES and activations.shape[0] == LEN:
        everything, features = gather(activations, cotangents, in_factor, out_factor, earlier)
    else:
        everything = lax.all_gather(earlier, AXES, axis=0, tiled=True)
        features = plain_features(activations, cotangents, in_factor, out_factor)
    gram, features = gram_of(everything, features)
    return features, gram


def solution(mesh):
    rows = P(("dom", "fsdp", "dp"), None)
    return jax.shard_map(
        on_device,
        mesh=mesh,
        in_specs=(rows, rows, P(), P(), rows),
        out_specs=(rows, rows),
        check_vma=False,
    )
```

```python
import functools

import jax
import jax.numpy as jnp
from jax import lax
from jax.experimental import pallas as pl
from jax.experimental.pallas import tpu as pltpu
from jax.sharding import PartitionSpec as P

LEN = 128
AXES = ("fsdp", "dp")
MIB = 1 << 20
CHUNKS = 4
AHEAD = 8
LAG = 0.5
PIECES = 16
GATHER_VMEM = 52 * MIB
GRAM_VMEM = 28 * MIB
DEPTH = 4
SIDES = 2


def plan():
    last, half = DEPTH - 1, range(CHUNKS // 2)
    whole = range(CHUNKS)
    queue = {}
    for z in range(DEPTH):
        if z < last:
            queue[z, "up"] = [(0, s, k) for s in range(z, -1, -1) for k in whole] + [(1, 0, k) for k in half]
        if z > 0:
            queue[z, "down"] = [(0, s, k) for s in range(z, DEPTH) for k in whole] + [(1, last, k) for k in half]
        queue[z, "side"] = [(0, s, k) for d in range(DEPTH) for k in whole for s in sorted({z - d, z + d})
                            if 0 <= s <= last and (s == z or s not in (0, last) or k not in half)]
    here = {(z, (0, z, k)): 0.0 for z in range(DEPTH) for k in whole}
    free = dict.fromkeys(queue, 0.0)
    left = {q: list(items) for q, items in queue.items()}
    order = {q: [] for q in queue}
    while any(left.values()):
        at, q, p = min((max(free[q], here[q[0], p]), q, n) for q, items in left.items()
                       for n, p in enumerate(items) if (q[0], p) in here)
        p = left[q].pop(p)
        free[q] = at + 1
        order[q].append((at + 1, p))
        z, link = q
        to, line = {"up": (z + 1, p[0]), "down": (z - 1, p[0]), "side": (z, 1 - p[0])}[link]
        here[to, (line, *p[1:])] = at + 1 + LAG

    programs = []
    for z in range(DEPTH):
        events = [(0.0, 1, ("start", "core", (0, z, k))) for k in whole] + [(0.0, 2, ("features", None, None))]
        for (to, p), at in here.items():
            if to == z and p[:2] != (0, z):
                events += [(at, 3, ("arrived", "side", p)), (at, 5, ("start", "core", p))]
        for link in ("up", "down", "side"):
            done = order.get((z, link), [])
            for n, (end, p) in enumerate(done):
                before = done[n - AHEAD] if n >= AHEAD else (0.0, None)
                at = max(here[z, p], before[0])
                if before[1] is not None:
                    events.append((at, 4, ("sent", link, before[1])))
                events.append((at, 0 if at == 0 else 4, ("start", link, p)))
        steps = [step for _, _, step in sorted(events, key=lambda e: e[:2])]
        waited = {s[1:] for s in steps if s[0] == "sent"}
        steps += [("sent", *s[1:]) for s in steps if s[0] == "start" and s[1:] not in waited]
        programs.append(steps)
    return programs


def gather_kernel(act_ref, cot_ref, inf_ref, outf_ref, own_ref, all_ref, feat_ref,
                  act, cot, inf, outf, flat, blk, up_sem, down_sem, side_sem, core_sem,
                  ici_sem, pair_sem, own_sem, load_sem):
    dom, f, c = lax.axis_index("dom"), lax.axis_index("fsdp"), lax.axis_index("dp")
    z, y = f // SIDES, f % SIDES
    rows, width = own_ref.shape
    step = width // CHUNKS
    last = DEPTH - 1

    def device(zz, yy, cc):
        return (dom, zz * SIDES + yy, cc)

    up, down = device(jnp.minimum(z + 1, last), y, c), device(jnp.maximum(z - 1, 0), y, c)
    side, pair = device(z, 1 - y, c), device(z, y, 1 - c)
    has_up, has_down = z < last, z > 0

    loads = [pltpu.make_async_copy(s, d, load_sem.at[i])
             for i, (s, d) in enumerate(((act_ref, act), (cot_ref, cot), (inf_ref, inf), (outf_ref, outf)))]
    for copy in loads:
        copy.start()

    barrier = pltpu.get_barrier_semaphore()

    def greet(to):
        pl.semaphore_signal(barrier, inc=1, device_id=to, device_id_type=pl.DeviceIdType.MESH)

    pl.when(has_up)(lambda: greet(up))
    pl.when(has_down)(lambda: greet(down))
    greet(side)
    greet(pair)
    pl.semaphore_wait(barrier, 2 + has_up.astype(jnp.int32) + has_down.astype(jnp.int32))

    def place(ff, cc, k):
        start = pl.multiple_of((ff * 2 + cc) * rows, rows)
        return all_ref.at[pl.ds(start, rows), pl.ds(k * step, step)]

    keep = pltpu.make_async_copy(own_ref, all_ref.at[pl.ds(pl.multiple_of((f * 2 + c) * rows, rows), rows)], own_sem)
    keep.start()

    def features():
        for copy in loads:
            copy.wait()
        kin, kout = inf.shape[0], outf.shape[1]
        part = width // 8

        def project(i, totals):
            at = pl.ds(pl.multiple_of(i * part, part), part)
            return (totals[0] + lax.dot_general(act[:, at], inf[:, at], (((1,), (1,)), ((), ())), preferred_element_type=jnp.float32),
                    totals[1] + jnp.dot(cot[:, at], outf[at, :], preferred_element_type=jnp.float32))

        inner, outer = lax.fori_loop(0, 8, project, (jnp.zeros((LEN, kin), jnp.float32), jnp.zeros((LEN, kout), jnp.float32)))
        inner, outer = inner.astype(jnp.bfloat16), outer.astype(jnp.bfloat16)
        blk[...] = lax.dot_general(outer, inner, (((0,), (0,)), ((), ())), preferred_element_type=jnp.float32) * LEN ** (-0.5)
        wide = jnp.concatenate([blk[pl.ds(0, kout // 2, 2), :], blk[pl.ds(1, kout // 2, 2), :]], axis=1)
        for a in range(kout // 2):
            flat[0:1, 2 * kin * a:2 * kin * (a + 1)] = wide[a:a + 1, :]
        feat_ref[...] = flat[...].astype(feat_ref.dtype)

    links = {"up": (up_sem, up), "down": (down_sem, down), "side": (side_sem, side), "core": (core_sem, pair)}

    def run(row, program):
        def remote(link, piece):
            line, source, k = piece
            ff = source * SIDES + (y if line == 0 else 1 - y)
            sems, to = links[link]
            src = own_ref.at[:, pl.ds(k * step, step)] if (line, source) == (0, row) else place(ff, c, k)
            return pltpu.make_async_remote_copy(
                src_ref=src, dst_ref=place(ff, c, k), send_sem=sems.at[ff, k],
                recv_sem=(pair_sem if link == "core" else ici_sem).at[ff, k],
                device_id=to, device_id_type=pl.DeviceIdType.MESH)

        for what, link, piece in program:
            if what == "features":
                features()
            elif what == "start":
                remote(link, piece).start()
            elif what == "sent":
                remote(link, piece).wait_send()
            else:
                remote(link, piece).wait_recv()

    for row, program in enumerate(plan()):
        pl.when(z == row)(functools.partial(run, row, program))

    keep.wait()
    for ff in range(DEPTH * SIDES):
        for k in range(CHUNKS):
            pltpu.make_async_remote_copy(
                src_ref=place(ff, 1 - c, k), dst_ref=place(ff, 1 - c, k), send_sem=core_sem.at[ff, k],
                recv_sem=pair_sem.at[ff, k], device_id=pair, device_id_type=pl.DeviceIdType.MESH).wait_recv()


def gather(activations, cotangents, in_factor, out_factor, earlier):
    rows, width = earlier.shape
    devices = DEPTH * SIDES * 2
    kin, kout = in_factor.shape[1], out_factor.shape[1]
    hbm = pl.BlockSpec(memory_space=pltpu.HBM)
    dma = pltpu.SemaphoreType.DMA
    chips = DEPTH * SIDES
    return pl.pallas_call(
        gather_kernel,
        name="gather_and_features",
        out_shape=(pltpu.VMEM((rows * devices, width), earlier.dtype),
                   pltpu.VMEM((1, kin * kout), jnp.bfloat16)),
        in_specs=[hbm] * 5,
        out_specs=(pl.BlockSpec(memory_space=pl.ANY), pl.BlockSpec(memory_space=pltpu.VMEM)),
        scratch_shapes=[
            pltpu.VMEM(activations.shape, activations.dtype),
            pltpu.VMEM(cotangents.shape, cotangents.dtype),
            pltpu.VMEM(in_factor.shape[::-1], in_factor.dtype),
            pltpu.VMEM(out_factor.shape, out_factor.dtype),
            pltpu.VMEM((1, kin * kout), jnp.float32),
            pltpu.VMEM((kout, kin), jnp.float32),
            *[dma((chips, CHUNKS))] * 6,
            dma(()),
            dma((4,)),
        ],
        compiler_params=pltpu.CompilerParams(collective_id=1, has_side_effects=True, vmem_limit_bytes=GATHER_VMEM),
    )(activations, cotangents, in_factor.T, out_factor, earlier)


def gram_kernel(scale, all_ref, feat_ref, gram_ref, out_feat_ref, turned, tiles, sems):
    owned, width = gram_ref.shape
    pieces = PIECES
    tile = width // pieces
    me = lax.axis_index("fsdp") * lax.axis_size("dp") + lax.axis_index("dp")
    out_feat_ref[...] = feat_ref[...]
    turned[...] = all_ref[:, pl.ds(pl.multiple_of(me * owned, owned), owned)].T
    copies = []
    for j in range(pieces):
        at = pl.ds(j * tile, tile)
        tiles[:, at] = jnp.dot(turned[...], all_ref[:, at], preferred_element_type=jnp.float32) * scale
        copies.append(pltpu.make_async_copy(tiles.at[:, at], gram_ref.at[:, at], sems.at[j]))
        copies[-1].start()
    for copy in copies:
        copy.wait()


def gram_of(everything, features):
    total, width = everything.shape
    assert total & (total - 1) == 0
    owned = width // (lax.axis_size("fsdp") * lax.axis_size("dp"))
    vmem = pl.BlockSpec(memory_space=pltpu.VMEM)
    return pl.pallas_call(
        functools.partial(gram_kernel, 1.0 / total),
        name="gram",
        out_shape=(jax.ShapeDtypeStruct((owned, width), jnp.float32),
                   jax.ShapeDtypeStruct(features.shape, features.dtype)),
        in_specs=[vmem, vmem],
        out_specs=(pl.BlockSpec(memory_space=pl.ANY), vmem),
        scratch_shapes=[pltpu.VMEM((owned, total), everything.dtype),
                        pltpu.VMEM((owned, width), jnp.float32),
                        pltpu.SemaphoreType.DMA((PIECES,))],
        compiler_params=pltpu.CompilerParams(vmem_limit_bytes=GRAM_VMEM),
    )(everything, features)


def plain_features(activations, cotangents, in_factor, out_factor):
    inner = jnp.dot(activations, in_factor, preferred_element_type=jnp.float32).astype(jnp.bfloat16)
    outer = jnp.dot(cotangents, out_factor, preferred_element_type=jnp.float32).astype(jnp.bfloat16)
    kin, kout = inner.shape[1], outer.shape[1]
    blocks = jnp.einsum("sta,stb->sab", outer.reshape(-1, LEN, kout), inner.reshape(-1, LEN, kin),
                        preferred_element_type=jnp.float32)
    return (blocks.reshape(-1, kout * kin) * LEN ** (-0.5)).astype(jnp.bfloat16)


def plain_gram(earlier):
    everything = lax.all_gather(earlier, AXES, axis=0, tiled=True)
    total, width = everything.shape
    devices = lax.axis_size("fsdp") * lax.axis_size("dp")
    owned = width // devices
    me = lax.axis_index("fsdp") * lax.axis_size("dp") + lax.axis_index("dp")
    cols = lax.dynamic_slice_in_dim(everything, me * owned, owned, 1)
    return lax.dot_general(cols, everything, (((0,), (0,)), ((), ())), preferred_element_type=jnp.float32) / total


def on_device(activations, cotangents, in_factor, out_factor, earlier):
    if lax.axis_size("fsdp") == DEPTH * SIDES and activations.shape[0] == LEN:
        everything, features = gather(activations, cotangents, in_factor, out_factor, earlier)
        gram, features = gram_of(everything, features)
        return features, gram
    return plain_features(activations, cotangents, in_factor, out_factor), plain_gram(earlier)


def solution(mesh):
    rows = P(("dom", "fsdp", "dp"), None)
    return jax.shard_map(
        on_device,
        mesh=mesh,
        in_specs=(rows, rows, P(), P(), rows),
        out_specs=(rows, rows),
        check_vma=False,
    )
```

```python
import functools

import jax
import jax.numpy as jnp
from jax import lax
from jax.experimental import pallas as pl
from jax.experimental.pallas import tpu as pltpu
from jax.sharding import PartitionSpec as P

LEN = 128
AXES = ("fsdp", "dp")
MIB = 1 << 20
CHUNKS = 4
AHEAD = 8
LAG = 0.5
PIECES = 16
GATHER_VMEM = 52 * MIB
GRAM_VMEM = 28 * MIB
DEPTH = 4
SIDES = 2


def plan():
    last, half = DEPTH - 1, range(CHUNKS // 2)
    whole = range(CHUNKS)
    queue = {}
    for z in range(DEPTH):
        if z < last:
            queue[z, "up"] = [(0, s, k) for s in range(z, -1, -1) for k in whole] + [(1, 0, k) for k in half]
        if z > 0:
            queue[z, "down"] = [(0, s, k) for s in range(z, DEPTH) for k in whole] + [(1, last, k) for k in half]
        queue[z, "side"] = [(0, s, k) for d in range(DEPTH) for k in whole for s in sorted({z - d, z + d})
                            if 0 <= s <= last and (s == z or s not in (0, last) or k not in half)]
    here = {(z, (0, z, k)): 0.0 for z in range(DEPTH) for k in whole}
    free = dict.fromkeys(queue, 0.0)
    left = {q: list(items) for q, items in queue.items()}
    order = {q: [] for q in queue}
    while any(left.values()):
        at, q, p = min((max(free[q], here[q[0], p]), q, n) for q, items in left.items()
                       for n, p in enumerate(items) if (q[0], p) in here)
        p = left[q].pop(p)
        free[q] = at + 1
        order[q].append((at + 1, p))
        z, link = q
        to, line = {"up": (z + 1, p[0]), "down": (z - 1, p[0]), "side": (z, 1 - p[0])}[link]
        here[to, (line, *p[1:])] = at + 1 + LAG

    programs = []
    for z in range(DEPTH):
        events = [(0.0, 1, ("start", "core", (0, z, k))) for k in whole] + [(0.0, 2, ("features", None, None))]
        for (to, p), at in here.items():
            if to == z and p[:2] != (0, z):
                events += [(at, 3, ("arrived", "side", p)), (at, 5, ("start", "core", p))]
        for link in ("up", "down", "side"):
            done = order.get((z, link), [])
            for n, (end, p) in enumerate(done):
                before = done[n - AHEAD] if n >= AHEAD else (0.0, None)
                at = max(here[z, p], before[0])
                if before[1] is not None:
                    events.append((at, 4, ("sent", link, before[1])))
                events.append((at, 0 if at == 0 else 4, ("start", link, p)))
        steps = [step for _, _, step in sorted(events, key=lambda e: e[:2])]
        waited = {s[1:] for s in steps if s[0] == "sent"}
        steps += [("sent", *s[1:]) for s in steps if s[0] == "start" and s[1:] not in waited]
        programs.append(steps)
    return programs


def gather_kernel(act_ref, cot_ref, inf_ref, outf_ref, own_ref, all_ref, feat_ref,
                  act, cot, inf, outf, flat, blk, up_sem, down_sem, side_sem, core_sem,
                  ici_sem, pair_sem, own_sem, load_sem):
    dom, f, c = lax.axis_index("dom"), lax.axis_index("fsdp"), lax.axis_index("dp")
    z, y = f // SIDES, f % SIDES
    rows, width = own_ref.shape
    step = width // CHUNKS
    last = DEPTH - 1

    def device(zz, yy, cc):
        return (dom, zz * SIDES + yy, cc)

    up, down = device(jnp.minimum(z + 1, last), y, c), device(jnp.maximum(z - 1, 0), y, c)
    side, pair = device(z, 1 - y, c), device(z, y, 1 - c)
    has_up, has_down = z < last, z > 0

    loads = [pltpu.make_async_copy(s, d, load_sem.at[i])
             for i, (s, d) in enumerate(((act_ref, act), (cot_ref, cot), (inf_ref, inf), (outf_ref, outf)))]
    barrier = pltpu.get_barrier_semaphore()

    def greet(to):
        pl.semaphore_signal(barrier, inc=1, device_id=to, device_id_type=pl.DeviceIdType.MESH)

    pl.when(has_up)(lambda: greet(up))
    pl.when(has_down)(lambda: greet(down))
    greet(side)
    greet(pair)
    for copy in loads:
        copy.start()
    pl.semaphore_wait(barrier, 2 + has_up.astype(jnp.int32) + has_down.astype(jnp.int32))

    def place(ff, cc, k):
        start = pl.multiple_of((ff * 2 + cc) * rows, rows)
        return all_ref.at[pl.ds(start, rows), pl.ds(k * step, step)]

    keep = pltpu.make_async_copy(own_ref, all_ref.at[pl.ds(pl.multiple_of((f * 2 + c) * rows, rows), rows)], own_sem)

    def features():
        for copy in loads:
            copy.wait()
        kin, kout = inf.shape[0], outf.shape[1]
        part = width // 8

        def project(i, totals):
            at = pl.ds(pl.multiple_of(i * part, part), part)
            return (totals[0] + lax.dot_general(act[:, at], inf[:, at], (((1,), (1,)), ((), ())), preferred_element_type=jnp.float32),
                    totals[1] + jnp.dot(cot[:, at], outf[at, :], preferred_element_type=jnp.float32))

        inner, outer = lax.fori_loop(0, 8, project, (jnp.zeros((LEN, kin), jnp.float32), jnp.zeros((LEN, kout), jnp.float32)))
        inner, outer = inner.astype(jnp.bfloat16), outer.astype(jnp.bfloat16)
        blk[...] = lax.dot_general(outer, inner, (((0,), (0,)), ((), ())), preferred_element_type=jnp.float32) * LEN ** (-0.5)
        wide = jnp.concatenate([blk[pl.ds(0, kout // 2, 2), :], blk[pl.ds(1, kout // 2, 2), :]], axis=1)
        for a in range(kout // 2):
            flat[0:1, 2 * kin * a:2 * kin * (a + 1)] = wide[a:a + 1, :]
        feat_ref[...] = flat[...].astype(feat_ref.dtype)

    links = {"up": (up_sem, up), "down": (down_sem, down), "side": (side_sem, side), "core": (core_sem, pair)}

    def run(row, program):
        def remote(link, piece):
            line, source, k = piece
            ff = source * SIDES + (y if line == 0 else 1 - y)
            sems, to = links[link]
            src = own_ref.at[:, pl.ds(k * step, step)] if (line, source) == (0, row) else place(ff, c, k)
            return pltpu.make_async_remote_copy(
                src_ref=src, dst_ref=place(ff, c, k), send_sem=sems.at[ff, k],
                recv_sem=(pair_sem if link == "core" else ici_sem).at[ff, k],
                device_id=to, device_id_type=pl.DeviceIdType.MESH)

        for what, link, piece in program:
            if what == "features":
                keep.start()
                features()
            elif what == "start":
                remote(link, piece).start()
            elif what == "sent":
                remote(link, piece).wait_send()
            else:
                remote(link, piece).wait_recv()

    for row, program in enumerate(plan()):
        pl.when(z == row)(functools.partial(run, row, program))

    keep.wait()
    for ff in range(DEPTH * SIDES):
        for k in range(CHUNKS):
            pltpu.make_async_remote_copy(
                src_ref=place(ff, 1 - c, k), dst_ref=place(ff, 1 - c, k), send_sem=core_sem.at[ff, k],
                recv_sem=pair_sem.at[ff, k], device_id=pair, device_id_type=pl.DeviceIdType.MESH).wait_recv()


def gather(activations, cotangents, in_factor, out_factor, earlier):
    rows, width = earlier.shape
    devices = DEPTH * SIDES * 2
    kin, kout = in_factor.shape[1], out_factor.shape[1]
    hbm = pl.BlockSpec(memory_space=pltpu.HBM)
    dma = pltpu.SemaphoreType.DMA
    chips = DEPTH * SIDES
    return pl.pallas_call(
        gather_kernel,
        name="gather_and_features",
        out_shape=(pltpu.VMEM((rows * devices, width), earlier.dtype),
                   pltpu.VMEM((1, kin * kout), jnp.bfloat16)),
        in_specs=[hbm] * 5,
        out_specs=(pl.BlockSpec(memory_space=pl.ANY), pl.BlockSpec(memory_space=pltpu.VMEM)),
        scratch_shapes=[
            pltpu.VMEM(activations.shape, activations.dtype),
            pltpu.VMEM(cotangents.shape, cotangents.dtype),
            pltpu.VMEM(in_factor.shape[::-1], in_factor.dtype),
            pltpu.VMEM(out_factor.shape, out_factor.dtype),
            pltpu.VMEM((1, kin * kout), jnp.float32),
            pltpu.VMEM((kout, kin), jnp.float32),
            *[dma((chips, CHUNKS))] * 6,
            dma(()),
            dma((4,)),
        ],
        compiler_params=pltpu.CompilerParams(collective_id=1, has_side_effects=True, vmem_limit_bytes=GATHER_VMEM),
    )(activations, cotangents, in_factor.T, out_factor, earlier)


def gram_kernel(scale, all_ref, feat_ref, gram_ref, out_feat_ref, turned, tiles, sems):
    owned, width = gram_ref.shape
    pieces = PIECES
    tile = width // pieces
    me = lax.axis_index("fsdp") * lax.axis_size("dp") + lax.axis_index("dp")
    out_feat_ref[...] = feat_ref[...]
    turned[...] = all_ref[:, pl.ds(pl.multiple_of(me * owned, owned), owned)].T
    copies = []
    for j in range(pieces):
        at = pl.ds(j * tile, tile)
        tiles[:, at] = jnp.dot(turned[...], all_ref[:, at], preferred_element_type=jnp.float32) * scale
        copies.append(pltpu.make_async_copy(tiles.at[:, at], gram_ref.at[:, at], sems.at[j]))
        copies[-1].start()
    for copy in copies:
        copy.wait()


def gram_of(everything, features):
    total, width = everything.shape
    assert total & (total - 1) == 0
    owned = width // (lax.axis_size("fsdp") * lax.axis_size("dp"))
    vmem = pl.BlockSpec(memory_space=pltpu.VMEM)
    return pl.pallas_call(
        functools.partial(gram_kernel, 1.0 / total),
        name="gram",
        out_shape=(jax.ShapeDtypeStruct((owned, width), jnp.float32),
                   jax.ShapeDtypeStruct(features.shape, features.dtype)),
        in_specs=[vmem, vmem],
        out_specs=(pl.BlockSpec(memory_space=pl.ANY), vmem),
        scratch_shapes=[pltpu.VMEM((owned, total), everything.dtype),
                        pltpu.VMEM((owned, width), jnp.float32),
                        pltpu.SemaphoreType.DMA((PIECES,))],
        compiler_params=pltpu.CompilerParams(vmem_limit_bytes=GRAM_VMEM),
    )(everything, features)


def plain_features(activations, cotangents, in_factor, out_factor):
    inner = jnp.dot(activations, in_factor, preferred_element_type=jnp.float32).astype(jnp.bfloat16)
    outer = jnp.dot(cotangents, out_factor, preferred_element_type=jnp.float32).astype(jnp.bfloat16)
    kin, kout = inner.shape[1], outer.shape[1]
    blocks = jnp.einsum("sta,stb->sab", outer.reshape(-1, LEN, kout), inner.reshape(-1, LEN, kin),
                        preferred_element_type=jnp.float32)
    return (blocks.reshape(-1, kout * kin) * LEN ** (-0.5)).astype(jnp.bfloat16)


def plain_gram(earlier):
    everything = lax.all_gather(earlier, AXES, axis=0, tiled=True)
    total, width = everything.shape
    devices = lax.axis_size("fsdp") * lax.axis_size("dp")
    owned = width // devices
    me = lax.axis_index("fsdp") * lax.axis_size("dp") + lax.axis_index("dp")
    cols = lax.dynamic_slice_in_dim(everything, me * owned, owned, 1)
    return lax.dot_general(cols, everything, (((0,), (0,)), ((), ())), preferred_element_type=jnp.float32) / total


def on_device(activations, cotangents, in_factor, out_factor, earlier):
    if lax.axis_size("fsdp") == DEPTH * SIDES and activations.shape[0] == LEN:
        everything, features = gather(activations, cotangents, in_factor, out_factor, earlier)
        gram, features = gram_of(everything, features)
        return features, gram
    return plain_features(activations, cotangents, in_factor, out_factor), plain_gram(earlier)


def solution(mesh):
    rows = P(("dom", "fsdp", "dp"), None)
    return jax.shard_map(
        on_device,
        mesh=mesh,
        in_specs=(rows, rows, P(), P(), rows),
        out_specs=(rows, rows),
        check_vma=False,
    )
```
